32 devices in a mesh: region: 4 (over y, core), var: 8 (over z, x).
Axes of the slice: x: 2, y: 2, z: 4, core: 2. Of those that a mesh axis runs over, the one named last changes fastest.
Arguments:
- state: float32 [16384, 768], P(('region', 'var')), may hold values from -6 to 6
- taper: bfloat16 [4, 16384, 384], P(None, ('region', 'var')), may hold values from 0.19921875 to 1
- block_mask: int32 [4, 128, 3], P(None, ('region', 'var')), may hold values 0 or 1
- anom_fly: float32 [4, 384, 768], P('region', 'var'), may hold values from -6 to 6
- incr_fly: float32 [4, 384, 768], P('region', 'var'), may hold values from -6 to 6
- anom_new: float32 [3, 384, 768], P(None, 'var'), may hold values from -6 to 6
- incr_new: float32 [3, 384, 768], P(None, 'var'), may hold values from -6 to 6
Outputs:
- updated: float32 [16384, 768], P(('region', 'var'))
The draws below stay inside these ranges and needn't reach their ends.
All inputs are finite; a program needn't handle non-finite values. No bound on the sum of `block_mask` on one device may be relied on, other than what follows from the above.
Results may differ from the reference program's by a relative error of at most 0.0003.
Values sent between devices are 32-bit elements; how exact they have to be, the bound alone decides.
A program may use at most 64 MiB of HBM per device.

```python
import jax
import jax.numpy as jnp
from jax import lax

MEMBERS = 768
OBS = 384
BLOCK = 128
TICKS = 4
ROWS_DEV = 512
ROWS = 16384
NEWB = 3
N_REGION = 4
N_VAR = 8


def touch_ends(values, stream_key, least, high):
    spot = [jax.random.randint(jax.random.fold_in(stream_key, axis), (), 0, length) for axis, length in enumerate(values.shape)]
    main_axis = values.shape.index(max(values.shape))
    neighbour = spot[:main_axis] + [(spot[main_axis] + 1) % values.shape[main_axis]] + spot[main_axis + 1:]
    return values.at[tuple(spot)].set(least).at[tuple(neighbour)].set(high)


def block_scale(stream_key, dims, pieces, smallest, high):
    factor_of = 1.0
    for axis_at, blocks in pieces:
        draws = jax.random.uniform(jax.random.fold_in(jax.random.fold_in(stream_key, 6), axis_at), (blocks,), jnp.float32, smallest / len(pieces), high / len(pieces))
        factor_of = factor_of * jnp.repeat(jnp.exp(draws), dims[axis_at] // blocks).reshape((-1,) + (1,) * (len(dims) - 1 - axis_at))
    return factor_of


def noise(stream_key, dims, scale, bound, split=(), held_as=jnp.bfloat16):
    entries = scale * jax.random.normal(stream_key, dims, jnp.float32)
    if split:
        entries = entries * block_scale(stream_key, dims, split, -0.22, 0.18)
    return jnp.clip(entries, -bound, bound).astype(held_as)


def setup_inputs(seed: int = 0) -> dict:
    key_list = jax.random.split(jax.random.key(seed), 8)
    state = noise(key_list[0], (ROWS, MEMBERS), 1.0, 6.0, ((0, 32),), jnp.float32)
    taper = jnp.clip(0.19921875 + 0.80078125 * jax.random.uniform(key_list[1], (TICKS, ROWS, OBS), jnp.float32) ** block_scale(key_list[1], (TICKS, ROWS, OBS), ((1, 32),), -0.2, 0.2), 0.19921875, 1.0).astype(jnp.bfloat16)
    block_mask = touch_ends((jax.random.randint(key_list[2], (TICKS, ROWS // BLOCK, OBS // BLOCK), 0, 2) < 1).astype(jnp.int32), jax.random.fold_in(key_list[2], 1), 0, 1)
    anom_fly = noise(key_list[3], (N_REGION, OBS, MEMBERS), 1.0, 6.0, ((0, 4), (1, 8)), jnp.float32)
    incr_fly = noise(key_list[4], (N_REGION, OBS, MEMBERS), 1.0, 6.0, ((0, 4), (1, 8)), jnp.float32)
    anom_new = noise(key_list[5], (NEWB, OBS, MEMBERS), 1.0, 6.0, ((1, 8),), jnp.float32)
    incr_new = noise(key_list[6], (NEWB, OBS, MEMBERS), 1.0, 6.0, ((1, 8),), jnp.float32)
    return dict(state=state, taper=taper, block_mask=block_mask, anom_fly=anom_fly, incr_fly=incr_fly, anom_new=anom_new, incr_new=incr_new)


def reference(state, taper, block_mask, anom_fly, incr_fly, anom_new, incr_new):
    span = N_VAR * ROWS_DEV
    all_anom = jnp.concatenate([anom_fly[::-1], anom_new], 0)
    all_incr = jnp.concatenate([incr_fly[::-1], incr_new], 0)

    def one_region(region_id):
        state_rows = lax.dynamic_slice_in_dim(state, region_id * span, span, 0)
        for tick_num in range(TICKS):
            batch_num = (N_REGION - 1 + tick_num) - region_id
            anomaly = lax.dynamic_index_in_dim(all_anom, batch_num, 0, keepdims=False)
            increment_rows = lax.dynamic_index_in_dim(all_incr, batch_num, 0, keepdims=False)
            local_taper = lax.dynamic_slice_in_dim(taper[tick_num], region_id * span, span, 0).astype(jnp.float32)
            block_flags = lax.dynamic_slice_in_dim(block_mask[tick_num], region_id * (span // BLOCK), span // BLOCK, 0)
            expanded = jnp.repeat(jnp.repeat(block_flags, BLOCK, 0), BLOCK, 1).astype(jnp.float32)
            covar = jnp.dot(state_rows, anomaly.T, precision=lax.Precision.HIGHEST, preferred_element_type=jnp.float32)
            weights = local_taper * expanded * covar / (MEMBERS - 1)
            state_rows = state_rows + jnp.dot(weights, increment_rows, precision=lax.Precision.HIGHEST, preferred_element_type=jnp.float32)
        return state_rows

    regions = lax.map(one_region, jnp.arange(N_REGION, dtype=jnp.int32))
    return regions.reshape(N_REGION * span, MEMBERS)
```

```python
import functools
import math

import jax
import jax.numpy as jnp
from jax import lax
from jax.experimental import pallas as pl
from jax.experimental.pallas import tpu as pltpu
from jax.sharding import PartitionSpec as P

MESH = pl.DeviceIdType.MESH
CORES = 2
PARTS = 2
ORDER = {
    (0, 0): (0, 1, 2, 3, 4),
    (0, 1): (3, 0, 4, 1, 2),
    (1, 0): (0, 1, 2, 3, 4),
    (1, 1): (2, 0, 3, 1, 4),
}
NT = (((1,), (1,)), ((), ()))
NN = (((1,), (0,)), ((), ()))


def split(value):
    high = value.astype(jnp.bfloat16)
    return high, (value - high.astype(jnp.float32)).astype(jnp.bfloat16)


def dot3(left, right_high, right_low, dims):
    high, low = split(left)
    rows = left.shape[0]
    both = lax.dot_general(
        jnp.concatenate([high, low], 0), right_high, dims, preferred_element_type=jnp.float32
    )
    cross = lax.dot_general(high, right_low, dims, preferred_element_type=jnp.float32)
    return both[:rows] + (both[rows:] + cross)


def kernel(
    n_region, n_var, n_x, ticks,
    mask_ref, state_ref, taper_ref, anom_fly, incr_fly, anom_new, incr_new,
    out_ref,
    buf, y_high, y_low, d_high, d_low, stage, recv, sent, seed_sent,
):
    slots = ticks + 1
    n_y, n_z = n_region // CORES, n_var // n_x
    region, var = lax.axis_index("region"), lax.axis_index("var")
    y, core = region // CORES, region % CORES
    z, x = var // n_x, var % n_x
    odd = y % 2
    fly, new = (anom_fly, incr_fly), (anom_new, incr_new)
    members = state_ref.shape[1]
    shard = buf.shape[3]
    block = state_ref.shape[0] // mask_ref.shape[1]

    def pick(table):
        return jnp.where(
            odd == 0,
            jnp.where(core == 0, table[0, 0], table[0, 1]),
            jnp.where(core == 0, table[1, 0], table[1, 1]),
        )

    def is_common(parity, slot):
        return jnp.where(parity == 0, slot <= ticks - 2, slot >= 2)

    def is_plane(parity, part, slot):
        return jnp.logical_or(jnp.logical_not(is_common(parity, slot)), parity == part)

    barrier = pltpu.get_barrier_semaphore()
    greeted = jnp.int32(0)
    reach = min(2, n_y - 1)
    others = [(z + 1 < n_z, region, var + n_x), (z > 0, region, var - n_x),
              (x + 1 < n_x, region, var + 1), (x > 0, region, var - 1)]
    for dy in range(-reach, reach + 1):
        for c in range(CORES):
            here = jnp.logical_and(y + dy >= 0, y + dy < n_y)
            target = (y + dy) * CORES + c
            others.append((jnp.logical_and(here, target != region), target, var))
    for there, r, v in others:
        @pl.when(there)
        def _(r=r, v=v):
            pl.semaphore_signal(barrier, inc=1, device_id=(r, v), device_id_type=MESH)
        greeted = greeted + there.astype(jnp.int32)
    pl.semaphore_wait(barrier, greeted)

    def seeds(begin):
        for dy in range(0, reach + 1):
            for part in range(PARTS):
                slot = 2 * dy + 1 - core
                target = (y + dy) * CORES + part
                go = jnp.logical_and(slot < slots, is_plane((y + dy) % 2, part, slot))
                go = jnp.logical_and(go, y + dy < n_y)
                go = jnp.logical_and(go, target != region)

                @pl.when(go)
                def _(part=part, slot=slot, target=target, dy=dy):
                    copy = pltpu.make_async_remote_copy(
                        src_ref=fly[part].at[0],
                        dst_ref=buf.at[slot, part, var],
                        send_sem=seed_sent.at[dy, part],
                        recv_sem=recv.at[slot, part, var],
                        device_id=(target, var),
                        device_id_type=MESH,
                    )
                    if begin:
                        copy.start()
                    else:
                        copy.wait_send()

    for slot in range(slots):
        batch = 2 * y + 1 - slot
        for part in range(PARTS):
            mine = jnp.logical_and(core == part, is_plane(odd, part, slot))

            @pl.when(jnp.logical_and(mine, batch == region))
            def _(slot=slot, part=part):
                pltpu.make_async_copy(
                    fly[part].at[0], buf.at[slot, part, var], recv.at[slot, part, var]
                ).start()

            if slot >= 2:
                @pl.when(jnp.logical_and(mine, batch < 0))
                def _(slot=slot, part=part, batch=batch):
                    pltpu.make_async_copy(
                        new[part].at[jnp.maximum(-batch - 1, 0)],
                        buf.at[slot, part, var],
                        recv.at[slot, part, var],
                    ).start()
    seeds(True)

    def wait_item(slot, part, source):
        here = buf.at[slot, part, source]
        pltpu.make_async_copy(here, here, recv.at[slot, part, source]).wait()

    def copies(unit, slot, z_from, x_from, act):
        source = z_from * n_x + x_from
        plane = is_plane(odd, core, slot)
        x_first = jnp.logical_and(odd != core, slot == jnp.where(odd == 0, slots - 1, 1))
        along_z = jnp.logical_and(plane, jnp.logical_or(x_first, x_from == x))
        along_x = jnp.logical_and(
            plane, jnp.logical_or(jnp.logical_not(x_first), z_from == z)
        )
        up = jnp.logical_and(z_from <= z, z + 1 < n_z)
        down = jnp.logical_and(z_from >= z, z > 0)
        right = jnp.logical_and(x_from <= x, x + 1 < n_x)
        left = jnp.logical_and(x_from >= x, x > 0)
        across = jnp.logical_and(plane, is_common(odd, slot))
        near = jnp.where(core == 0, slot < slots - 1, slot > 0)
        routes = [
            (jnp.logical_and(along_z, up), region, var + n_x, slot),
            (jnp.logical_and(along_z, down), region, var - n_x, slot),
            (jnp.logical_and(along_x, right), region, var + 1, slot),
            (jnp.logical_and(along_x, left), region, var - 1, slot),
            (across, region + CORES * (1 - 2 * odd), var, slot + 2 * (1 - 2 * odd)),
            (near, region + 1 - 2 * core, var, slot),
        ]
        for way, (go, r, v, slot_there) in enumerate(routes):
            @pl.when(go)
            def _(way=way, r=r, v=v, slot_there=slot_there):
                act(pltpu.make_async_remote_copy(
                    src_ref=buf.at[slot, core, source],
                    dst_ref=buf.at[slot_there, core, source],
                    send_sem=sent.at[unit, source, way],
                    recv_sem=recv.at[slot_there, core, source],
                    device_id=(r, v),
                    device_id_type=MESH,
                ))

    def begin(copy):
        copy.start()

    def end(copy):
        copy.wait_send()

    def handle(unit, slot, z_from, x_from):
        wait_item(slot, core, z_from * n_x + x_from)
        copies(unit, slot, z_from, x_from, begin)

    def own(unit, want_plane):
        slot = pick({key: order[unit] for key, order in ORDER.items()})
        plane = is_plane(odd, core, slot)

        @pl.when(plane if want_plane else jnp.logical_not(plane))
        def _():
            handle(unit, slot, z, x)

    def items(unit, first, last):
        slot = pick({key: order[unit] for key, order in ORDER.items()})

        def body(n, carry):
            k = n // n_x
            far = (k + 1) // 2
            z_from = z + jnp.where(k % 2 == 1, far, -far)
            x_from = (x + n % n_x) % n_x

            @pl.when(jnp.logical_and(z_from >= 0, z_from < n_z))
            def _():
                handle(unit, slot, z_from, x_from)
            return carry

        lax.fori_loop(first, last, body, 0)

    n_items = (2 * n_z - 1) * n_x
    n_chunks = mask_ref.shape[1]

    def prepare(tick):
        slot = tick + 1 - core

        def arrive(source, carry):
            wait_item(slot, 1 - core, source)
            return carry

        lax.fori_loop(0, n_var, arrive, 0)
        for part, high, low in ((0, y_high, y_low), (1, d_high, d_low)):
            if shard % 16 == 0:
                def cut(source, carry, part=part, high=high, low=low):
                    rows = pl.ds(pl.multiple_of(source * shard, 16), shard)
                    high[rows, :], low[rows, :] = split(buf[slot, part, source])
                    return carry

                lax.fori_loop(0, n_var, cut, 0)
            else:
                for source in range(n_var):
                    stage[pl.ds(source * shard, shard), :] = buf[slot, part, source]
                high[...], low[...] = split(stage[...])

    def chunk(tick, c):
        rows = pl.ds(pl.multiple_of(c * block, block), block)
        rows_in = out_ref[rows, :]
        covar = dot3(rows_in, y_high[...], y_low[...], NT)
        taper_now = taper_ref[tick, rows, :].astype(jnp.float32)
        n_obs_blocks = mask_ref.shape[2]
        width = covar.shape[1] // n_obs_blocks
        pieces = []
        for b in range(n_obs_blocks):
            flag = mask_ref[tick, c, b].astype(jnp.float32) * (1.0 / (members - 1))
            cols = slice(b * width, (b + 1) * width)
            pieces.append(taper_now[:, cols] * covar[:, cols] * flag)
        weights = jnp.concatenate(pieces, 1)
        out_ref[rows, :] = rows_in + dot3(weights, d_high[...], d_low[...], NN)

    def tick_now(tick):
        prepare(tick)

        def body(c, carry):
            chunk(tick, c)
            return carry

        lax.fori_loop(0, n_chunks, body, 0)

    out_ref[...] = state_ref[...]
    own(0, True)
    for unit in range(slots):
        if unit + 1 < slots:
            own(unit + 1, True)
        own(unit, False)
        if unit == slots - 1:
            prepare(0)

            def mixed(c, carry):
                chunk(0, c)
                return carry

            edges = [1 + (n_items - 1) * c // n_chunks for c in range(n_chunks + 1)]
            for c in range(n_chunks):
                items(unit, edges[c], edges[c + 1])
                lax.fori_loop(c, c + 1, mixed, 0)
        else:
            items(unit, 1, n_items)
    lax.fori_loop(1, ticks, lambda tick, carry: (tick_now(tick), carry)[1], 0)

    seeds(False)
    for unit in range(slots):
        slot = pick({key: order[unit] for key, order in ORDER.items()})

        def body(source, carry, unit=unit, slot=slot):
            copies(unit, slot, source // n_x, source % n_x, end)
            return carry

        lax.fori_loop(0, n_var, body, 0)


def on_device(n_region, n_var, state, taper, block_mask, anom_fly, incr_fly, anom_new, incr_new):
    ticks = taper.shape[0]
    shard, members = anom_fly.shape[1:]
    obs = shard * n_var
    n_x = 2 ** (int(math.log2(n_var)) // 2)
    slots = ticks + 1
    vmem = pl.BlockSpec(memory_space=pltpu.VMEM)
    anywhere = pl.BlockSpec(memory_space=pl.ANY)
    flops = 3 * 4 * ticks * state.shape[0] * obs * members
    return pl.pallas_call(
        functools.partial(kernel, n_region, n_var, n_x, ticks),
        out_shape=jax.ShapeDtypeStruct(state.shape, jnp.float32),
        in_specs=[pl.BlockSpec(memory_space=pltpu.SMEM), vmem, vmem] + [anywhere] * 4,
        out_specs=vmem,
        scratch_shapes=[
            pltpu.VMEM((slots, PARTS, n_var, shard, members), jnp.float32),
            pltpu.VMEM((obs, members), jnp.bfloat16),
            pltpu.VMEM((obs, members), jnp.bfloat16),
            pltpu.VMEM((obs, members), jnp.bfloat16),
            pltpu.VMEM((obs, members), jnp.bfloat16),
            pltpu.VMEM((8, 128) if shard % 16 == 0 else (obs, members), jnp.float32),
            pltpu.SemaphoreType.DMA((slots, PARTS, n_var)),
            pltpu.SemaphoreType.DMA((slots, n_var, 6)),
            pltpu.SemaphoreType.DMA((3, PARTS)),
        ],
        compiler_params=pltpu.CompilerParams(
            collective_id=0, has_side_effects=True, vmem_limit_bytes=48 * 1024 * 1024
        ),
        cost_estimate=pl.CostEstimate(
            flops=flops, bytes_accessed=4 * state.size * 4, transcendentals=0
        ),
        name="gather_and_assimilate",
    )(block_mask, state, taper, anom_fly, incr_fly, anom_new, incr_new)


def solution(mesh):
    n_region, n_var = mesh.shape["region"], mesh.shape["var"]
    in_specs = (
        P(("region", "var"), None),
        P(None, ("region", "var"), None),
        P(None, ("region", "var"), None),
        P("region", "var", None),
        P("region", "var", None),
        P(None, "var", None),
        P(None, "var", None),
    )
    out_specs = P(("region", "var"), None)
    return jax.shard_map(
        functools.partial(on_device, n_region, n_var),
        mesh=mesh, in_specs=in_specs, out_specs=out_specs, check_vma=False,
    )
```

```python
import functools
import math

import jax
import jax.numpy as jnp
from jax import lax
from jax.experimental import pallas as pl
from jax.experimental.pallas import tpu as pltpu
from jax.sharding import PartitionSpec as P

MESH = pl.DeviceIdType.MESH
CORES = 2
PARTS = 2
UNITS = {
    (0, 0): ((0, 0), (1, 0), (2, 0), (3, 0)),
    (0, 1): ((3, 1), (4, 1), (4, 0)),
    (1, 0): ((0, 0), (0, 1), (1, 0), (1, 1)),
    (1, 1): ((2, 1), (3, 1), (4, 1)),
}
N_UNITS = 4
N_SHARED = 3
AHEAD = 2
NT = (((1,), (1,)), ((), ()))
NN = (((1,), (0,)), ((), ()))


def split(value):
    high = value.astype(jnp.bfloat16)
    return high, (value - high.astype(jnp.float32)).astype(jnp.bfloat16)


def dot3(left, right_high, right_low, dims):
    high, low = split(left)
    rows = left.shape[0]
    both = lax.dot_general(
        jnp.concatenate([high, low], 0), right_high, dims, preferred_element_type=jnp.float32
    )
    cross = lax.dot_general(high, right_low, dims, preferred_element_type=jnp.float32)
    return both[:rows] + (both[rows:] + cross)


def kernel(
    n_region, n_var, n_x, ticks,
    mask_ref, state_ref, taper_hbm, anom_fly, incr_fly, anom_new, incr_new,
    out_ref,
    buf, taper_ref, y_high, y_low, d_high, d_low, stage, recv, sent, seed_sent, load,
):
    slots = ticks + 1
    n_y, n_z = n_region // CORES, n_var // n_x
    region, var = lax.axis_index("region"), lax.axis_index("var")
    y, core = region // CORES, region % CORES
    z, x = var // n_x, var % n_x
    odd = y % 2
    fly, new = (anom_fly, incr_fly), (anom_new, incr_new)
    members = state_ref.shape[1]
    shard = buf.shape[3]
    block = state_ref.shape[0] // mask_ref.shape[1]

    state_load = pltpu.make_async_copy(state_ref, out_ref, load.at[0])
    taper_load = pltpu.make_async_copy(taper_hbm, taper_ref, load.at[1])
    state_load.start()
    taper_load.start()

    def choose(parity, mate, table):
        return jnp.where(
            parity == 0,
            jnp.where(mate == 0, table[0, 0], table[0, 1]),
            jnp.where(mate == 0, table[1, 0], table[1, 1]),
        )

    def is_carried(parity, mate, slot, part):
        def listed(pairs):
            found = False
            for unit_slot, unit_part in pairs:
                if unit_part == part:
                    found = jnp.logical_or(found, slot == unit_slot)
            return jnp.asarray(found)
        return choose(parity, mate, {key: listed(pairs) for key, pairs in UNITS.items()})

    def is_shared(parity, slot):
        return jnp.where(parity == 0, slot < N_SHARED, slot >= slots - N_SHARED)

    def carrier(slot, part):
        here = jnp.logical_and(is_shared(odd, slot), odd != part)
        return jnp.where(
            is_carried(odd, 0, slot, part), 0, jnp.where(here, part, 1)
        )

    barrier = pltpu.get_barrier_semaphore()
    greeted = jnp.int32(0)
    reach = min(2, n_y - 1)
    others = [(z + 1 < n_z, region, var + n_x), (z > 0, region, var - n_x),
              (x + 1 < n_x, region, var + 1), (x > 0, region, var - 1)]
    for dy in range(-reach, reach + 1):
        for c in range(CORES):
            here = jnp.logical_and(y + dy >= 0, y + dy < n_y)
            target = (y + dy) * CORES + c
            others.append((jnp.logical_and(here, target != region), target, var))
    for there, r, v in others:
        @pl.when(there)
        def _(r=r, v=v):
            pl.semaphore_signal(barrier, inc=1, device_id=(r, v), device_id_type=MESH)
        greeted = greeted + there.astype(jnp.int32)
    pl.semaphore_wait(barrier, greeted)

    def seeds(begin):
        for dy in range(0, reach + 1):
            for mate in range(CORES):
                slot = 2 * dy + 1 - core
                target = (y + dy) * CORES + mate
                for part in range(PARTS):
                    go = jnp.logical_and(
                        slot < slots, is_carried((y + dy) % 2, mate, slot, part)
                    )
                    go = jnp.logical_and(go, y + dy < n_y)
                    go = jnp.logical_and(go, target != region)

                    @pl.when(go)
                    def _(part=part, slot=slot, target=target, dy=dy, mate=mate):
                        copy = pltpu.make_async_remote_copy(
                            src_ref=fly[part].at[0],
                            dst_ref=buf.at[slot, part, var],
                            send_sem=seed_sent.at[dy, mate, part],
                            recv_sem=recv.at[slot, part, var],
                            device_id=(target, var),
                            device_id_type=MESH,
                        )
                        if begin:
                            copy.start()
                        else:
                            copy.wait_send()

    for slot in range(slots):
        batch = 2 * y + 1 - slot
        for part in range(PARTS):
            mine = is_carried(odd, core, slot, part)

            @pl.when(jnp.logical_and(mine, batch == region))
            def _(slot=slot, part=part):
                pltpu.make_async_copy(
                    fly[part].at[0], buf.at[slot, part, var], recv.at[slot, part, var]
                ).start()

            if slot >= 2:
                @pl.when(jnp.logical_and(mine, batch < 0))
                def _(slot=slot, part=part, batch=batch):
                    pltpu.make_async_copy(
                        new[part].at[jnp.maximum(-batch - 1, 0)],
                        buf.at[slot, part, var],
                        recv.at[slot, part, var],
                    ).start()
    seeds(True)

    def wait_item(slot, part, source):
        here = buf.at[slot, part, source]
        pltpu.make_async_copy(here, here, recv.at[slot, part, source]).wait()

    def plane_unit(unit):
        pairs = {key: units[min(unit, len(units) - 1)] for key, units in UNITS.items()}
        slot = choose(odd, core, {key: pair[0] for key, pair in pairs.items()})
        part = choose(odd, core, {key: pair[1] for key, pair in pairs.items()})
        there = choose(odd, core, {key: unit < len(units) for key, units in UNITS.items()})
        return slot, part, there

    def shared_unit(unit):
        return unit + (slots - N_SHARED) * odd, 1 - odd, core != odd

    def near_copy(slot, part, source, send_sem, act):
        @pl.when(jnp.where(core == 0, slot < slots - 1, slot > 0))
        def _():
            act(pltpu.make_async_remote_copy(
                src_ref=buf.at[slot, part, source],
                dst_ref=buf.at[slot, part, source],
                send_sem=send_sem,
                recv_sem=recv.at[slot, part, source],
                device_id=(region + 1 - 2 * core, var),
                device_id_type=MESH,
            ))

    def copies(unit, slot, part, z_from, x_from, act):
        source = z_from * n_x + x_from
        x_first = jnp.where(
            odd == 0,
            jnp.logical_and(slot == slots - 1, part == 1),
            jnp.logical_and(slot == 1, part == 0),
        )
        along_z = jnp.logical_or(x_first, x_from == x)
        along_x = jnp.logical_or(jnp.logical_not(x_first), z_from == z)
        up = jnp.logical_and(z_from <= z, z + 1 < n_z)
        down = jnp.logical_and(z_from >= z, z > 0)
        right = jnp.logical_and(x_from <= x, x + 1 < n_x)
        left = jnp.logical_and(x_from >= x, x > 0)
        across = is_shared(odd, slot)
        routes = [
            (jnp.logical_and(along_z, up), region, var + n_x, slot),
            (jnp.logical_and(along_z, down), region, var - n_x, slot),
            (jnp.logical_and(along_x, right), region, var + 1, slot),
            (jnp.logical_and(along_x, left), region, var - 1, slot),
            (across, region + CORES * (1 - 2 * odd), var, slot + 2 * (1 - 2 * odd)),
        ]
        for way, (go, r, v, slot_there) in enumerate(routes):
            @pl.when(go)
            def _(way=way, r=r, v=v, slot_there=slot_there):
                act(pltpu.make_async_remote_copy(
                    src_ref=buf.at[slot, part, source],
                    dst_ref=buf.at[slot_there, part, source],
                    send_sem=sent.at[unit, source, way],
                    recv_sem=recv.at[slot_there, part, source],
                    device_id=(r, v),
                    device_id_type=MESH,
                ))
        near_copy(slot, part, source, sent.at[unit, source, len(routes)], act)

    def begin(copy):
        copy.start()

    def end(copy):
        copy.wait_send()

    def ring(hop, act):
        pairs = [
            (dz, dx)
            for ax in range(min(hop, n_x - 1) + 1)
            for dz in sorted({hop - ax, ax - hop}, reverse=True)
            for dx in sorted({ax, -ax}, reverse=True)
            if hop - ax < n_z
        ]
        for dz, dx in pairs:
            z_from, x_from = z + dz, x + dx
            inside = jnp.logical_and(z_from >= 0, z_from < n_z)
            inside = jnp.logical_and(inside, jnp.logical_and(x_from >= 0, x_from < n_x))

            @pl.when(inside)
            def _(z_from=z_from, x_from=x_from):
                act(z_from, x_from)

    def gather_step(unit, hop):
        slot, part, there = plane_unit(unit)

        def handle(z_from, x_from):
            wait_item(slot, part, z_from * n_x + x_from)
            copies(unit, slot, part, z_from, x_from, begin)

        @pl.when(there)
        def _():
            ring(hop, handle)

    def shared_step(unit, hop):
        slot, part, there = shared_unit(unit)

        def handle(z_from, x_from):
            source = z_from * n_x + x_from
            wait_item(slot, part, source)
            near_copy(slot, part, source, sent.at[N_UNITS + unit, source, 0], begin)

        @pl.when(there)
        def _():
            ring(hop, handle)

    per_chunk = 2 if mask_ref.shape[1] % 2 == 0 else 1
    n_chunks = mask_ref.shape[1] // per_chunk
    height = per_chunk * block

    def prepare(tick):
        slot = tick + 1 - core

        for part in range(PARTS):
            def arrive(source, carry, part=part):
                wait_item(slot, part, source)
                return carry

            @pl.when(carrier(slot, part) != core)
            def _(arrive=arrive):
                lax.fori_loop(0, n_var, arrive, 0)

        for part, high, low in ((0, y_high, y_low), (1, d_high, d_low)):
            if shard % 16 == 0:
                def cut(source, carry, part=part, high=high, low=low):
                    rows = pl.ds(pl.multiple_of(source * shard, 16), shard)
                    high[rows, :], low[rows, :] = split(buf[slot, part, source])
                    return carry

                lax.fori_loop(0, n_var, cut, 0)
            else:
                for source in range(n_var):
                    stage[pl.ds(source * shard, shard), :] = buf[slot, part, source]
                high[...], low[...] = split(stage[...])

    def chunk(tick, c):
        rows = pl.ds(pl.multiple_of(c * height, height), height)
        rows_in = out_ref[rows, :]
        covar = dot3(rows_in, y_high[...], y_low[...], NT)
        taper_now = taper_ref[tick, rows, :].astype(jnp.float32)
        n_obs_blocks = mask_ref.shape[2]
        width = covar.shape[1] // n_obs_blocks
        strips = []
        for a in range(per_chunk):
            lines = slice(a * block, (a + 1) * block)
            pieces = []
            for b in range(n_obs_blocks):
                flag = mask_ref[tick, c * per_chunk + a, b].astype(jnp.float32)
                flag = flag * (1.0 / (members - 1))
                cols = slice(b * width, (b + 1) * width)
                pieces.append(taper_now[lines, cols] * covar[lines, cols] * flag)
            strips.append(jnp.concatenate(pieces, 1))
        weights = jnp.concatenate(strips, 0)
        out_ref[rows, :] = rows_in + dot3(weights, d_high[...], d_low[...], NN)

    def tick_now(tick):
        prepare(tick)

        def body(c, carry):
            chunk(tick, c)
            return carry

        lax.fori_loop(0, n_chunks, body, 0)

    far = n_z + n_x - 2
    last_step = N_UNITS - 1 + far
    early = jnp.logical_or(odd == 0, core == 1)
    for unit in range(AHEAD):
        gather_step(unit, 0)
    for step in range(last_step + 1):
        if step + AHEAD < N_UNITS:
            gather_step(step + AHEAD, 0)
        for unit in range(N_UNITS):
            if 1 <= step - unit <= far:
                gather_step(unit, step - unit)
        for unit in range(N_SHARED):
            if 0 <= step - unit - 1 <= far:
                shared_step(unit, step - unit - 1)
        if step == last_step - 1:
            state_load.wait()
            taper_load.wait()

            @pl.when(early)
            def _():
                tick_now(0)

    def later(tick, carry):
        tick_now(tick)
        return carry

    lax.fori_loop(early.astype(jnp.int32), ticks, later, 0)

    seeds(False)
    for unit in range(N_UNITS):
        slot, part, there = plane_unit(unit)

        def left(source, carry, unit=unit, slot=slot, part=part):
            copies(unit, slot, part, source // n_x, source % n_x, end)
            return carry

        @pl.when(there)
        def _(left=left):
            lax.fori_loop(0, n_var, left, 0)
    for unit in range(N_SHARED):
        slot, part, there = shared_unit(unit)

        def gone(source, carry, unit=unit, slot=slot, part=part):
            near_copy(slot, part, source, sent.at[N_UNITS + unit, source, 0], end)
            return carry

        @pl.when(there)
        def _(gone=gone):
            lax.fori_loop(0, n_var, gone, 0)


def on_device(n_region, n_var, state, taper, block_mask, anom_fly, incr_fly, anom_new, incr_new):
    ticks = taper.shape[0]
    shard, members = anom_fly.shape[1:]
    obs = shard * n_var
    n_x = 2 ** (int(math.log2(n_var)) // 2)
    slots = ticks + 1
    vmem = pl.BlockSpec(memory_space=pltpu.VMEM)
    anywhere = pl.BlockSpec(memory_space=pl.ANY)
    flops = 3 * 4 * ticks * state.shape[0] * obs * members
    return pl.pallas_call(
        functools.partial(kernel, n_region, n_var, n_x, ticks),
        out_shape=jax.ShapeDtypeStruct(state.shape, jnp.float32),
        in_specs=[pl.BlockSpec(memory_space=pltpu.SMEM)] + [anywhere] * 6,
        out_specs=vmem,
        scratch_shapes=[
            pltpu.VMEM((slots, PARTS, n_var, shard, members), jnp.float32),
            pltpu.VMEM(taper.shape, taper.dtype),
            pltpu.VMEM((obs, members), jnp.bfloat16),
            pltpu.VMEM((obs, members), jnp.bfloat16),
            pltpu.VMEM((obs, members), jnp.bfloat16),
            pltpu.VMEM((obs, members), jnp.bfloat16),
            pltpu.VMEM((8, 128) if shard % 16 == 0 else (obs, members), jnp.float32),
            pltpu.SemaphoreType.DMA((slots, PARTS, n_var)),
            pltpu.SemaphoreType.DMA((N_UNITS + N_SHARED, n_var, 6)),
            pltpu.SemaphoreType.DMA((3, CORES, PARTS)),
            pltpu.SemaphoreType.DMA((2,)),
        ],
        compiler_params=pltpu.CompilerParams(
            collective_id=0, has_side_effects=True, vmem_limit_bytes=60 * 1024 * 1024
        ),
        cost_estimate=pl.CostEstimate(
            flops=flops, bytes_accessed=4 * state.size * 4, transcendentals=0
        ),
        name="gather_and_assimilate",
    )(block_mask, state, taper, anom_fly, incr_fly, anom_new, incr_new)


def solution(mesh):
    n_region, n_var = mesh.shape["region"], mesh.shape["var"]
    in_specs = (
        P(("region", "var"), None),
        P(None, ("region", "var"), None),
        P(None, ("region", "var"), None),
        P("region", "var", None),
        P("region", "var", None),
        P(None, "var", None),
        P(None, "var", None),
    )
    out_specs = P(("region", "var"), None)
    return jax.shard_map(
        functools.partial(on_device, n_region, n_var),
        mesh=mesh, in_specs=in_specs, out_specs=out_specs, check_vma=False,
    )
```

```python
import functools
import math

import jax
import jax.numpy as jnp
from jax import lax
from jax.experimental import pallas as pl
from jax.experimental.pallas import tpu as pltpu
from jax.sharding import PartitionSpec as P

MESH = pl.DeviceIdType.MESH
CORES = 2
PARTS = 2
UNITS = {
    (0, 0): ((0, 0), (1, 0), (2, 0), (3, 0)),
    (0, 1): ((3, 1), (4, 1), (4, 0)),
    (1, 0): ((0, 0), (0, 1), (1, 0), (1, 1)),
    (1, 1): ((2, 1), (3, 1), (4, 1)),
}
N_UNITS = 4
N_SHARED = 3
AHEAD = 4
NT = (((1,), (1,)), ((), ()))
NN = (((1,), (0,)), ((), ()))


def dot(left, right, dims):
    return lax.dot_general(left, right, dims, preferred_element_type=jnp.float32)


def split(value):
    high = value.astype(jnp.bfloat16)
    return high, (value - high.astype(jnp.float32)).astype(jnp.bfloat16)


def kernel(
    n_region, n_var, n_x, ticks,
    mask_ref, state_ref, taper_hbm, anom_fly, incr_fly, anom_new, incr_new,
    out_ref,
    buf, taper_ref, halves, stage, recv, sent, seed_sent, load,
):
    slots = ticks + 1
    n_y, n_z = n_region // CORES, n_var // n_x
    far = n_z + n_x - 2
    region, var = lax.axis_index("region"), lax.axis_index("var")
    y, core = region // CORES, region % CORES
    z, x = var // n_x, var % n_x
    odd = y % 2
    fly, new = (anom_fly, incr_fly), (anom_new, incr_new)
    members = state_ref.shape[1]
    shard = buf.shape[3]
    obs = shard * n_var
    aligned = shard % 16 == 0
    block = state_ref.shape[0] // mask_ref.shape[1]

    state_load = pltpu.make_async_copy(state_ref, out_ref, load.at[0])
    taper_load = pltpu.make_async_copy(taper_hbm, taper_ref, load.at[1])
    state_load.start()
    taper_load.start()

    def choose(parity, mate, table):
        return jnp.where(
            parity == 0,
            jnp.where(mate == 0, table[0, 0], table[0, 1]),
            jnp.where(mate == 0, table[1, 0], table[1, 1]),
        )

    def is_carried(parity, mate, slot, part):
        def listed(pairs):
            found = False
            for unit_slot, unit_part in pairs:
                if unit_part == part:
                    found = jnp.logical_or(found, slot == unit_slot)
            return jnp.asarray(found)
        return choose(parity, mate, {key: listed(pairs) for key, pairs in UNITS.items()})

    def is_shared(parity, slot):
        return jnp.where(parity == 0, slot < N_SHARED, slot >= slots - N_SHARED)

    barrier = pltpu.get_barrier_semaphore()
    greeted = jnp.int32(0)
    reach = min(2, n_y - 1)
    others = [(z + 1 < n_z, region, var + n_x), (z > 0, region, var - n_x),
              (x + 1 < n_x, region, var + 1), (x > 0, region, var - 1)]
    for dy in range(-reach, reach + 1):
        for c in range(CORES):
            here = jnp.logical_and(y + dy >= 0, y + dy < n_y)
            target = (y + dy) * CORES + c
            others.append((jnp.logical_and(here, target != region), target, var))
    for there, r, v in others:
        @pl.when(there)
        def _(r=r, v=v):
            pl.semaphore_signal(barrier, inc=1, device_id=(r, v), device_id_type=MESH)
        greeted = greeted + there.astype(jnp.int32)
    pl.semaphore_wait(barrier, greeted)

    def seeds(begin):
        for dy in range(0, reach + 1):
            for mate in range(CORES):
                slot = 2 * dy + 1 - core
                target = (y + dy) * CORES + mate
                for part in range(PARTS):
                    go = jnp.logical_and(
                        slot < slots, is_carried((y + dy) % 2, mate, slot, part)
                    )
                    go = jnp.logical_and(go, y + dy < n_y)
                    go = jnp.logical_and(go, target != region)

                    @pl.when(go)
                    def _(part=part, slot=slot, target=target, dy=dy, mate=mate):
                        copy = pltpu.make_async_remote_copy(
                            src_ref=fly[part].at[0],
                            dst_ref=buf.at[slot, part, var],
                            send_sem=seed_sent.at[dy, mate, part],
                            recv_sem=recv.at[slot, part, var],
                            device_id=(target, var),
                            device_id_type=MESH,
                        )
                        if begin:
                            copy.start()
                        else:
                            copy.wait_send()

    for slot in range(slots):
        batch = 2 * y + 1 - slot
        for part in range(PARTS):
            mine = is_carried(odd, core, slot, part)

            @pl.when(jnp.logical_and(mine, batch == region))
            def _(slot=slot, part=part):
                pltpu.make_async_copy(
                    fly[part].at[0], buf.at[slot, part, var], recv.at[slot, part, var]
                ).start()

            if slot >= 2:
                @pl.when(jnp.logical_and(mine, batch < 0))
                def _(slot=slot, part=part, batch=batch):
                    pltpu.make_async_copy(
                        new[part].at[jnp.maximum(-batch - 1, 0)],
                        buf.at[slot, part, var],
                        recv.at[slot, part, var],
                    ).start()
    seeds(True)

    def wait_item(slot, part, source):
        here = buf.at[slot, part, source]
        pltpu.make_async_copy(here, here, recv.at[slot, part, source]).wait()

    def plane_unit(unit, mate):
        pairs = {key: units[min(unit, len(units) - 1)] for key, units in UNITS.items()}
        slot = choose(odd, mate, {key: pair[0] for key, pair in pairs.items()})
        part = choose(odd, mate, {key: pair[1] for key, pair in pairs.items()})
        there = choose(odd, mate, {key: unit < len(units) for key, units in UNITS.items()})
        return slot, part, there

    def shared_unit(unit, mate):
        return unit + (slots - N_SHARED) * odd, 1 - odd, mate != odd

    def keep(slot, part, source):
        if not aligned:
            return
        tick = slot - 1 + core

        @pl.when(jnp.logical_and(tick >= 0, tick < ticks))
        def _():
            high, low = split(buf[slot, part, source])
            start = pl.multiple_of(source * shard, 16)
            halves[tick, part, pl.ds(start, shard), :] = high
            halves[tick, part, pl.ds(start + obs, shard), :] = low

    def near_copy(slot, part, source, send_sem, act):
        @pl.when(jnp.where(core == 0, slot < slots - 1, slot > 0))
        def _():
            act(pltpu.make_async_remote_copy(
                src_ref=buf.at[slot, part, source],
                dst_ref=buf.at[slot, part, source],
                send_sem=send_sem,
                recv_sem=recv.at[slot, part, source],
                device_id=(region + 1 - 2 * core, var),
                device_id_type=MESH,
            ))

    def copies(unit, slot, part, z_from, x_from, act):
        source = z_from * n_x + x_from
        x_first = jnp.where(
            odd == 0,
            jnp.logical_and(slot == slots - 1, part == 1),
            jnp.logical_and(slot == 1, part == 0),
        )
        along_z = jnp.logical_or(x_first, x_from == x)
        along_x = jnp.logical_or(jnp.logical_not(x_first), z_from == z)
        up = jnp.logical_and(z_from <= z, z + 1 < n_z)
        down = jnp.logical_and(z_from >= z, z > 0)
        right = jnp.logical_and(x_from <= x, x + 1 < n_x)
        left = jnp.logical_and(x_from >= x, x > 0)
        across = is_shared(odd, slot)
        routes = [
            (jnp.logical_and(along_z, up), region, var + n_x, slot),
            (jnp.logical_and(along_z, down), region, var - n_x, slot),
            (jnp.logical_and(along_x, right), region, var + 1, slot),
            (jnp.logical_and(along_x, left), region, var - 1, slot),
            (across, region + CORES * (1 - 2 * odd), var, slot + 2 * (1 - 2 * odd)),
        ]
        for way, (go, r, v, slot_there) in enumerate(routes):
            @pl.when(go)
            def _(way=way, r=r, v=v, slot_there=slot_there):
                act(pltpu.make_async_remote_copy(
                    src_ref=buf.at[slot, part, source],
                    dst_ref=buf.at[slot_there, part, source],
                    send_sem=sent.at[unit, source, way],
                    recv_sem=recv.at[slot_there, part, source],
                    device_id=(r, v),
                    device_id_type=MESH,
                ))
        near_copy(slot, part, source, sent.at[unit, source, len(routes)], act)

    def begin(copy):
        copy.start()

    def end(copy):
        copy.wait_send()

    def ring(hop, act):
        pairs = [
            (dz, dx)
            for ax in range(min(hop, n_x - 1) + 1)
            for dz in sorted({hop - ax, ax - hop}, reverse=True)
            for dx in sorted({ax, -ax}, reverse=True)
            if hop - ax < n_z
        ]
        for dz, dx in pairs:
            z_from, x_from = z + dz, x + dx
            inside = jnp.logical_and(z_from >= 0, z_from < n_z)
            inside = jnp.logical_and(inside, jnp.logical_and(x_from >= 0, x_from < n_x))

            @pl.when(inside)
            def _(z_from=z_from, x_from=x_from):
                act(z_from, x_from)

    def gather_step(unit, hop):
        slot, part, there = plane_unit(unit, core)

        def handle(z_from, x_from):
            wait_item(slot, part, z_from * n_x + x_from)
            copies(unit, slot, part, z_from, x_from, begin)
            keep(slot, part, z_from * n_x + x_from)

        @pl.when(there)
        def _():
            ring(hop, handle)

    def shared_step(unit, hop):
        slot, part, there = shared_unit(unit, core)

        def handle(z_from, x_from):
            source = z_from * n_x + x_from
            wait_item(slot, part, source)
            near_copy(slot, part, source, sent.at[N_UNITS + unit, source, 0], begin)
            keep(slot, part, source)

        @pl.when(there)
        def _():
            ring(hop, handle)

    def mate_step(step):
        for count, lag, which in ((N_UNITS, 0, plane_unit), (N_SHARED, 1, shared_unit)):
            for unit in range(count):
                hop = step - unit - lag
                if not 0 <= hop <= far:
                    continue
                slot, part, there = which(unit, 1 - core)
                needed = jnp.logical_and(slot - 1 + core >= 0, slot - 1 + core < ticks)

                def take(z_from, x_from, slot=slot, part=part):
                    source = z_from * n_x + x_from
                    wait_item(slot, part, source)
                    keep(slot, part, source)

                @pl.when(jnp.logical_and(there, needed))
                def _(hop=hop, take=take):
                    ring(hop, take)

    per_chunk = 2 if mask_ref.shape[1] % 2 == 0 else 1
    n_chunks = mask_ref.shape[1] // per_chunk
    height = per_chunk * block

    def prepare(tick):
        if aligned:
            return
        slot = tick + 1 - core
        for part in range(PARTS):
            for source in range(n_var):
                stage[pl.ds(source * shard, shard), :] = buf[slot, part, source]
            high, low = split(stage[...])
            halves[tick, part, :obs, :] = high
            halves[tick, part, obs:, :] = low

    def chunk(tick, c):
        rows = pl.ds(pl.multiple_of(c * height, height), height)
        rows_in = out_ref[rows, :]
        high, low = split(rows_in)
        pair = dot(high, halves[tick, 0], NT)
        covar = pair[:, :obs] + (pair[:, obs:] + dot(low, halves[tick, 0, :obs, :], NT))
        taper_now = taper_ref[tick, rows, :].astype(jnp.float32)
        n_obs_blocks = mask_ref.shape[2]
        width = covar.shape[1] // n_obs_blocks
        strips = []
        for a in range(per_chunk):
            lines = slice(a * block, (a + 1) * block)
            pieces = []
            for b in range(n_obs_blocks):
                flag = mask_ref[tick, c * per_chunk + a, b].astype(jnp.float32)
                flag = flag * (1.0 / (members - 1))
                cols = slice(b * width, (b + 1) * width)
                pieces.append(taper_now[lines, cols] * covar[lines, cols] * flag)
            strips.append(jnp.concatenate(pieces, 1))
        weights = jnp.concatenate(strips, 0)
        high, low = split(weights)
        gain = dot(jnp.concatenate([high, high], 1), halves[tick, 1], NN)
        out_ref[rows, :] = rows_in + (gain + dot(low, halves[tick, 1, :obs, :], NN))

    def tick_now(tick):
        prepare(tick)

        def body(c, carry):
            chunk(tick, c)
            return carry

        lax.fori_loop(0, n_chunks, body, 0)

    last_step = N_UNITS - 1 + far
    early = jnp.logical_or(odd == 0, core == 1)
    for unit in range(AHEAD):
        gather_step(unit, 0)
    for step in range(last_step + 1):
        if step + AHEAD < N_UNITS:
            gather_step(step + AHEAD, 0)
        for unit in range(N_UNITS):
            if 1 <= step - unit <= far:
                gather_step(unit, step - unit)
        for unit in range(N_SHARED):
            if 0 <= step - unit - 1 <= far:
                shared_step(unit, step - unit - 1)
        if 0 < step < last_step:
            mate_step(step - 1)
        if step == last_step - 1:
            mate_step(step)
            state_load.wait()
            taper_load.wait()

            @pl.when(early)
            def _():
                tick_now(0)
        elif step == last_step:
            mate_step(step)

    def later(tick, carry):
        tick_now(tick)
        return carry

    lax.fori_loop(early.astype(jnp.int32), ticks, later, 0)

    seeds(False)
    for unit in range(N_UNITS):
        slot, part, there = plane_unit(unit, core)

        def left(source, carry, unit=unit, slot=slot, part=part):
            copies(unit, slot, part, source // n_x, source % n_x, end)
            return carry

        @pl.when(there)
        def _(left=left):
            lax.fori_loop(0, n_var, left, 0)
    for unit in range(N_SHARED):
        slot, part, there = shared_unit(unit, core)

        def gone(source, carry, unit=unit, slot=slot, part=part):
            near_copy(slot, part, source, sent.at[N_UNITS + unit, source, 0], end)
            return carry

        @pl.when(there)
        def _(gone=gone):
            lax.fori_loop(0, n_var, gone, 0)


def on_device(n_region, n_var, state, taper, block_mask, anom_fly, incr_fly, anom_new, incr_new):
    ticks = taper.shape[0]
    shard, members = anom_fly.shape[1:]
    obs = shard * n_var
    n_x = 2 ** (int(math.log2(n_var)) // 2)
    slots = ticks + 1
    vmem = pl.BlockSpec(memory_space=pltpu.VMEM)
    anywhere = pl.BlockSpec(memory_space=pl.ANY)
    flops = 3 * 4 * ticks * state.shape[0] * obs * members
    return pl.pallas_call(
        functools.partial(kernel, n_region, n_var, n_x, ticks),
        out_shape=jax.ShapeDtypeStruct(state.shape, jnp.float32),
        in_specs=[pl.BlockSpec(memory_space=pltpu.SMEM)] + [anywhere] * 6,
        out_specs=vmem,
        scratch_shapes=[
            pltpu.VMEM((slots, PARTS, n_var, shard, members), jnp.float32),
            pltpu.VMEM(taper.shape, taper.dtype),
            pltpu.VMEM((ticks, PARTS, 2 * obs, members), jnp.bfloat16),
            pltpu.VMEM((8, 128) if shard % 16 == 0 else (obs, members), jnp.float32),
            pltpu.SemaphoreType.DMA((slots, PARTS, n_var)),
            pltpu.SemaphoreType.DMA((N_UNITS + N_SHARED, n_var, 6)),
            pltpu.SemaphoreType.DMA((3, CORES, PARTS)),
            pltpu.SemaphoreType.DMA((2,)),
        ],
        compiler_params=pltpu.CompilerParams(
            collective_id=0, has_side_effects=True, vmem_limit_bytes=60 * 1024 * 1024
        ),
        cost_estimate=pl.CostEstimate(
            flops=flops, bytes_accessed=4 * state.size * 4, transcendentals=0
        ),
        name="gather_and_assimilate",
    )(block_mask, state, taper, anom_fly, incr_fly, anom_new, incr_new)


def solution(mesh):
    n_region, n_var = mesh.shape["region"], mesh.shape["var"]
    in_specs = (
        P(("region", "var"), None),
        P(None, ("region", "var"), None),
        P(None, ("region", "var"), None),
        P("region", "var", None),
        P("region", "var", None),
        P(None, "var", None),
        P(None, "var", None),
    )
    out_specs = P(("region", "var"), None)
    return jax.shard_map(
        functools.partial(on_device, n_region, n_var),
        mesh=mesh, in_specs=in_specs, out_specs=out_specs, check_vma=False,
    )
```

```python
import functools
import math

import jax
import jax.numpy as jnp
from jax import lax
from jax.experimental import pallas as pl
from jax.experimental.pallas import tpu as pltpu
from jax.sharding import PartitionSpec as P

MESH = pl.DeviceIdType.MESH
CORES = 2
PARTS = 2
UNITS = {
    (0, 0): ((0, 0), (1, 0), (2, 0), (3, 0)),
    (0, 1): ((3, 1), (4, 1), (4, 0)),
    (1, 0): ((0, 0), (0, 1), (1, 0), (1, 1)),
    (1, 1): ((2, 1), (3, 1), (4, 1)),
}
N_UNITS = 4
N_SHARED = 3
AHEAD = 3
LAG = 3
NT = (((1,), (1,)), ((), ()))
NN = (((1,), (0,)), ((), ()))


def dot(left, right, dims):
    return lax.dot_general(left, right, dims, preferred_element_type=jnp.float32)


def split(value):
    high = value.astype(jnp.bfloat16)
    return high, (value - high.astype(jnp.float32)).astype(jnp.bfloat16)


def kernel(
    n_region, n_var, n_x, ticks,
    mask_hbm, state_ref, taper_hbm, anom_fly, incr_fly, anom_new, incr_new,
    out_ref,
    buf, taper_ref, mask_ref, halves, stage, recv, sent, seed_sent, load,
):
    slots = ticks + 1
    n_y, n_z = n_region // CORES, n_var // n_x
    far = n_z + n_x - 2
    region, var = lax.axis_index("region"), lax.axis_index("var")
    y, core = region // CORES, region % CORES
    z, x = var // n_x, var % n_x
    odd = y % 2
    fly, new = (anom_fly, incr_fly), (anom_new, incr_new)
    members = state_ref.shape[1]
    shard = buf.shape[3]
    obs = shard * n_var
    aligned = shard % 16 == 0
    block = state_ref.shape[0] // mask_ref.shape[1]

    state_load = pltpu.make_async_copy(state_ref, out_ref, load.at[0])
    taper_load = pltpu.make_async_copy(taper_hbm, taper_ref, load.at[1])
    mask_load = pltpu.make_async_copy(mask_hbm, mask_ref, load.at[2])
    mask_load.start()
    state_load.start()
    taper_load.start()

    def choose(parity, mate, table):
        return jnp.where(
            parity == 0,
            jnp.where(mate == 0, table[0, 0], table[0, 1]),
            jnp.where(mate == 0, table[1, 0], table[1, 1]),
        )

    def is_carried(parity, mate, slot, part):
        def listed(pairs):
            found = False
            for unit_slot, unit_part in pairs:
                if unit_part == part:
                    found = jnp.logical_or(found, slot == unit_slot)
            return jnp.asarray(found)
        return choose(parity, mate, {key: listed(pairs) for key, pairs in UNITS.items()})

    def is_shared(parity, slot):
        return jnp.where(parity == 0, slot < N_SHARED, slot >= slots - N_SHARED)

    barrier = pltpu.get_barrier_semaphore()
    greeted = jnp.int32(0)
    reach = min(2, n_y - 1)
    others = [(z + 1 < n_z, region, var + n_x), (z > 0, region, var - n_x),
              (x + 1 < n_x, region, var + 1), (x > 0, region, var - 1)]
    for dy in range(-reach, reach + 1):
        for c in range(CORES):
            here = jnp.logical_and(y + dy >= 0, y + dy < n_y)
            target = (y + dy) * CORES + c
            others.append((jnp.logical_and(here, target != region), target, var))
    for there, r, v in others:
        @pl.when(there)
        def _(r=r, v=v):
            pl.semaphore_signal(barrier, inc=1, device_id=(r, v), device_id_type=MESH)
        greeted = greeted + there.astype(jnp.int32)
    pl.semaphore_wait(barrier, greeted)

    def seeds(begin):
        for dy in range(0, reach + 1):
            for mate in range(CORES):
                slot = 2 * dy + 1 - core
                target = (y + dy) * CORES + mate
                for part in range(PARTS):
                    go = jnp.logical_and(
                        slot < slots, is_carried((y + dy) % 2, mate, slot, part)
                    )
                    go = jnp.logical_and(go, y + dy < n_y)
                    go = jnp.logical_and(go, target != region)

                    @pl.when(go)
                    def _(part=part, slot=slot, target=target, dy=dy, mate=mate):
                        copy = pltpu.make_async_remote_copy(
                            src_ref=fly[part].at[0],
                            dst_ref=buf.at[slot, part, var],
                            send_sem=seed_sent.at[dy, mate, part],
                            recv_sem=recv.at[slot, part, var],
                            device_id=(target, var),
                            device_id_type=MESH,
                        )
                        if begin:
                            copy.start()
                        else:
                            copy.wait_send()

    for slot in range(slots):
        batch = 2 * y + 1 - slot
        for part in range(PARTS):
            mine = is_carried(odd, core, slot, part)

            @pl.when(jnp.logical_and(mine, batch == region))
            def _(slot=slot, part=part):
                pltpu.make_async_copy(
                    fly[part].at[0], buf.at[slot, part, var], recv.at[slot, part, var]
                ).start()

            if slot >= 2:
                @pl.when(jnp.logical_and(mine, batch < 0))
                def _(slot=slot, part=part, batch=batch):
                    pltpu.make_async_copy(
                        new[part].at[jnp.maximum(-batch - 1, 0)],
                        buf.at[slot, part, var],
                        recv.at[slot, part, var],
                    ).start()
    seeds(True)

    def wait_item(slot, part, source):
        here = buf.at[slot, part, source]
        pltpu.make_async_copy(here, here, recv.at[slot, part, source]).wait()

    def plane_unit(unit, mate):
        pairs = {key: units[min(unit, len(units) - 1)] for key, units in UNITS.items()}
        slot = choose(odd, mate, {key: pair[0] for key, pair in pairs.items()})
        part = choose(odd, mate, {key: pair[1] for key, pair in pairs.items()})
        there = choose(odd, mate, {key: unit < len(units) for key, units in UNITS.items()})
        return slot, part, there

    def shared_unit(unit, mate):
        return unit + (slots - N_SHARED) * odd, 1 - odd, mate != odd

    def keep(slot, part, source):
        if not aligned:
            return
        tick = slot - 1 + core

        @pl.when(jnp.logical_and(tick >= 0, tick < ticks))
        def _():
            high, low = split(buf[slot, part, source])
            start = pl.multiple_of(source * shard, 16)
            halves[tick, part, pl.ds(start, shard), :] = high
            halves[tick, part, pl.ds(start + obs, shard), :] = low

    def near_copy(slot, part, source, send_sem, act):
        @pl.when(jnp.where(core == 0, slot < slots - 1, slot > 0))
        def _():
            act(pltpu.make_async_remote_copy(
                src_ref=buf.at[slot, part, source],
                dst_ref=buf.at[slot, part, source],
                send_sem=send_sem,
                recv_sem=recv.at[slot, part, source],
                device_id=(region + 1 - 2 * core, var),
                device_id_type=MESH,
            ))

    def copies(unit, slot, part, z_from, x_from, act):
        source = z_from * n_x + x_from
        x_first = jnp.where(
            odd == 0,
            jnp.logical_and(slot == slots - 1, part == 1),
            jnp.logical_and(slot == 1, part == 0),
        )
        along_z = jnp.logical_or(x_first, x_from == x)
        along_x = jnp.logical_or(jnp.logical_not(x_first), z_from == z)
        up = jnp.logical_and(z_from <= z, z + 1 < n_z)
        down = jnp.logical_and(z_from >= z, z > 0)
        right = jnp.logical_and(x_from <= x, x + 1 < n_x)
        left = jnp.logical_and(x_from >= x, x > 0)
        across = is_shared(odd, slot)
        routes = [
            (jnp.logical_and(along_z, up), region, var + n_x, slot),
            (jnp.logical_and(along_z, down), region, var - n_x, slot),
            (jnp.logical_and(along_x, right), region, var + 1, slot),
            (jnp.logical_and(along_x, left), region, var - 1, slot),
            (across, region + CORES * (1 - 2 * odd), var, slot + 2 * (1 - 2 * odd)),
        ]
        for way, (go, r, v, slot_there) in enumerate(routes):
            @pl.when(go)
            def _(way=way, r=r, v=v, slot_there=slot_there):
                act(pltpu.make_async_remote_copy(
                    src_ref=buf.at[slot, part, source],
                    dst_ref=buf.at[slot_there, part, source],
                    send_sem=sent.at[unit, source, way],
                    recv_sem=recv.at[slot_there, part, source],
                    device_id=(r, v),
                    device_id_type=MESH,
                ))
        near_copy(slot, part, source, sent.at[unit, source, len(routes)], act)

    def begin(copy):
        copy.start()

    def end(copy):
        copy.wait_send()

    def ring(hop, act):
        pairs = [
            (dz, dx)
            for ax in range(min(hop, n_x - 1) + 1)
            for dz in sorted({hop - ax, ax - hop}, reverse=True)
            for dx in sorted({ax, -ax}, reverse=True)
            if hop - ax < n_z
        ]
        for dz, dx in pairs:
            z_from, x_from = z + dz, x + dx
            inside = jnp.logical_and(z_from >= 0, z_from < n_z)
            inside = jnp.logical_and(inside, jnp.logical_and(x_from >= 0, x_from < n_x))

            @pl.when(inside)
            def _(z_from=z_from, x_from=x_from):
                act(z_from, x_from)

    def gather_step(unit, hop):
        slot, part, there = plane_unit(unit, core)

        def handle(z_from, x_from):
            wait_item(slot, part, z_from * n_x + x_from)
            copies(unit, slot, part, z_from, x_from, begin)

        @pl.when(there)
        def _():
            ring(hop, handle)

    def shared_step(unit, hop):
        slot, part, there = shared_unit(unit, core)

        def handle(z_from, x_from):
            source = z_from * n_x + x_from
            wait_item(slot, part, source)
            near_copy(slot, part, source, sent.at[N_UNITS + unit, source, 0], begin)

        @pl.when(there)
        def _():
            ring(hop, handle)

    def take_step(step, mate):
        for count, lag, which in ((N_UNITS, 0, plane_unit), (N_SHARED, 1, shared_unit)):
            for unit in range(count):
                hop = step - unit - lag
                if not 0 <= hop <= far:
                    continue
                slot, part, there = which(unit, mate)
                needed = jnp.logical_and(slot - 1 + core >= 0, slot - 1 + core < ticks)

                def take(z_from, x_from, slot=slot, part=part):
                    source = z_from * n_x + x_from
                    if mate is not core:
                        wait_item(slot, part, source)
                    keep(slot, part, source)

                @pl.when(jnp.logical_and(there, needed))
                def _(hop=hop, take=take):
                    ring(hop, take)

    per_chunk = 2 if mask_ref.shape[1] % 2 == 0 else 1
    n_chunks = mask_ref.shape[1] // per_chunk
    height = per_chunk * block

    def prepare(tick):
        if aligned:
            return
        slot = tick + 1 - core
        for part in range(PARTS):
            for source in range(n_var):
                stage[pl.ds(source * shard, shard), :] = buf[slot, part, source]
            high, low = split(stage[...])
            halves[tick, part, :obs, :] = high
            halves[tick, part, obs:, :] = low

    def chunk(tick, c):
        rows = pl.ds(pl.multiple_of(c * height, height), height)
        rows_in = out_ref[rows, :]
        high, low = split(rows_in)
        pair = dot(high, halves[tick, 0], NT)
        covar = pair[:, :obs] + (pair[:, obs:] + dot(low, halves[tick, 0, :obs, :], NT))
        taper_now = taper_ref[tick, rows, :].astype(jnp.float32)
        n_obs_blocks = mask_ref.shape[2]
        width = covar.shape[1] // n_obs_blocks
        strips = []
        for a in range(per_chunk):
            lines = slice(a * block, (a + 1) * block)
            pieces = []
            for b in range(n_obs_blocks):
                flag = mask_ref[tick, c * per_chunk + a, b].astype(jnp.float32)
                flag = flag * (1.0 / (members - 1))
                cols = slice(b * width, (b + 1) * width)
                pieces.append(taper_now[lines, cols] * covar[lines, cols] * flag)
            strips.append(jnp.concatenate(pieces, 1))
        weights = jnp.concatenate(strips, 0)
        high, low = split(weights)
        gain = dot(jnp.concatenate([high, high], 1), halves[tick, 1], NN)
        out_ref[rows, :] = rows_in + (gain + dot(low, halves[tick, 1, :obs, :], NN))

    def tick_now(tick):
        prepare(tick)

        def body(c, carry):
            chunk(tick, c)
            return carry

        lax.fori_loop(0, n_chunks, body, 0)

    last_step = N_UNITS - 1 + far
    other = 1 - core
    early = jnp.logical_or(odd == 0, core == 1)
    for unit in range(AHEAD):
        gather_step(unit, 0)
    for step in range(last_step + 1):
        if step + AHEAD < N_UNITS:
            gather_step(step + AHEAD, 0)
        for unit in range(N_UNITS):
            if 1 <= step - unit <= far:
                gather_step(unit, step - unit)
        for unit in range(N_SHARED):
            if 0 <= step - unit - 1 <= far:
                shared_step(unit, step - unit - 1)
        if 0 < step < last_step:
            take_step(step - 1, core)
        if LAG <= step < last_step - 1:
            take_step(step - LAG, other)
        if step == last_step - 1:
            take_step(step, core)
            for taken in range(step - LAG, last_step):
                take_step(taken, other)
            state_load.wait()
            taper_load.wait()
            mask_load.wait()

            @pl.when(early)
            def _():
                tick_now(0)
        elif step == last_step:
            take_step(step, core)
            take_step(step, other)

    def later(tick, carry):
        tick_now(tick)
        return carry

    lax.fori_loop(early.astype(jnp.int32), ticks, later, 0)

    seeds(False)
    for unit in range(N_UNITS):
        slot, part, there = plane_unit(unit, core)

        def left(source, carry, unit=unit, slot=slot, part=part):
            copies(unit, slot, part, source // n_x, source % n_x, end)
            return carry

        @pl.when(there)
        def _(left=left):
            lax.fori_loop(0, n_var, left, 0)
    for unit in range(N_SHARED):
        slot, part, there = shared_unit(unit, core)

        def gone(source, carry, unit=unit, slot=slot, part=part):
            near_copy(slot, part, source, sent.at[N_UNITS + unit, source, 0], end)
            return carry

        @pl.when(there)
        def _(gone=gone):
            lax.fori_loop(0, n_var, gone, 0)


def on_device(n_region, n_var, state, taper, block_mask, anom_fly, incr_fly, anom_new, incr_new):
    ticks = taper.shape[0]
    shard, members = anom_fly.shape[1:]
    obs = shard * n_var
    n_x = 2 ** (int(math.log2(n_var)) // 2)
    slots = ticks + 1
    vmem = pl.BlockSpec(memory_space=pltpu.VMEM)
    anywhere = pl.BlockSpec(memory_space=pl.ANY)
    flops = 3 * 4 * ticks * state.shape[0] * obs * members
    return pl.pallas_call(
        functools.partial(kernel, n_region, n_var, n_x, ticks),
        out_shape=jax.ShapeDtypeStruct(state.shape, jnp.float32),
        in_specs=[anywhere] * 7,
        out_specs=vmem,
        scratch_shapes=[
            pltpu.VMEM((slots, PARTS, n_var, shard, members), jnp.float32),
            pltpu.VMEM(taper.shape, taper.dtype),
            pltpu.SMEM(block_mask.shape, block_mask.dtype),
            pltpu.VMEM((ticks, PARTS, 2 * obs, members), jnp.bfloat16),
            pltpu.VMEM((8, 128) if shard % 16 == 0 else (obs, members), jnp.float32),
            pltpu.SemaphoreType.DMA((slots, PARTS, n_var)),
            pltpu.SemaphoreType.DMA((N_UNITS + N_SHARED, n_var, 6)),
            pltpu.SemaphoreType.DMA((3, CORES, PARTS)),
            pltpu.SemaphoreType.DMA((3,)),
        ],
        compiler_params=pltpu.CompilerParams(
            collective_id=0, has_side_effects=True, vmem_limit_bytes=60 * 1024 * 1024
        ),
        cost_estimate=pl.CostEstimate(
            flops=flops, bytes_accessed=4 * state.size * 4, transcendentals=0
        ),
        name="gather_and_assimilate",
    )(block_mask, state, taper, anom_fly, incr_fly, anom_new, incr_new)


def solution(mesh):
    n_region, n_var = mesh.shape["region"], mesh.shape["var"]
    in_specs = (
        P(("region", "var"), None),
        P(None, ("region", "var"), None),
        P(None, ("region", "var"), None),
        P("region", "var", None),
        P("region", "var", None),
        P(None, "var", None),
        P(None, "var", None),
    )
    out_specs = P(("region", "var"), None)
    return jax.shard_map(
        functools.partial(on_device, n_region, n_var),
        mesh=mesh, in_specs=in_specs, out_specs=out_specs, check_vma=False,
    )
```

```python
import functools
import math

import jax
import jax.numpy as jnp
from jax import lax
from jax.experimental import pallas as pl
from jax.experimental.pallas import tpu as pltpu
from jax.sharding import PartitionSpec as P

MESH = pl.DeviceIdType.MESH
CORES = 2
PARTS = 2
UNITS = {
    (0, 0): ((0, 0), (1, 0), (2, 0), (3, 0)),
    (0, 1): ((3, 1), (4, 1), (4, 0)),
    (1, 0): ((0, 0), (0, 1), (1, 0)),
    (1, 1): ((2, 1), (1, 1), (3, 1), (4, 1)),
}
N_UNITS = 4
N_SHARED = 3
AHEAD = 3
LAG = 3
NT = (((1,), (1,)), ((), ()))
NN = (((1,), (0,)), ((), ()))


def dot(left, right, dims):
    return lax.dot_general(left, right, dims, preferred_element_type=jnp.float32)


def split(value):
    high = value.astype(jnp.bfloat16)
    return high, (value - high.astype(jnp.float32)).astype(jnp.bfloat16)


def kernel(
    n_region, n_var, n_x, ticks,
    mask_hbm, state_ref, taper_hbm, anom_fly, incr_fly, anom_new, incr_new,
    out_ref,
    buf, taper_ref, mask_ref, ready, halves, stage, recv, sent, seed_sent, load,
):
    slots = ticks + 1
    n_y, n_z = n_region // CORES, n_var // n_x
    far = n_z + n_x - 2
    region, var = lax.axis_index("region"), lax.axis_index("var")
    y, core = region // CORES, region % CORES
    z, x = var // n_x, var % n_x
    odd = y % 2
    fly, new = (anom_fly, incr_fly), (anom_new, incr_new)
    members = state_ref.shape[1]
    shard = buf.shape[3]
    obs = shard * n_var
    aligned = shard % 16 == 0
    block = state_ref.shape[0] // mask_ref.shape[2]

    state_load = pltpu.make_async_copy(state_ref, out_ref, load.at[0])
    taper_load = pltpu.make_async_copy(taper_hbm, taper_ref, load.at[1])
    mask_load = pltpu.make_async_copy(mask_hbm, mask_ref, load.at[2])
    mask_load.start()
    state_load.start()
    taper_load.start()

    def choose(parity, mate, table):
        return jnp.where(
            parity == 0,
            jnp.where(mate == 0, table[0, 0], table[0, 1]),
            jnp.where(mate == 0, table[1, 0], table[1, 1]),
        )

    def is_carried(parity, mate, slot, part):
        def listed(pairs):
            found = False
            for unit_slot, unit_part in pairs:
                if unit_part == part:
                    found = jnp.logical_or(found, slot == unit_slot)
            return jnp.asarray(found)
        return choose(parity, mate, {key: listed(pairs) for key, pairs in UNITS.items()})

    def is_shared(parity, slot):
        return jnp.where(parity == 0, slot < N_SHARED, slot >= slots - N_SHARED)

    barrier = pltpu.get_barrier_semaphore()
    greeted = jnp.int32(0)
    reach = min(2, n_y - 1)
    others = [(z + 1 < n_z, region, var + n_x), (z > 0, region, var - n_x),
              (x + 1 < n_x, region, var + 1), (x > 0, region, var - 1)]
    for dy in range(-reach, reach + 1):
        for c in range(CORES):
            here = jnp.logical_and(y + dy >= 0, y + dy < n_y)
            target = (y + dy) * CORES + c
            others.append((jnp.logical_and(here, target != region), target, var))
    for there, r, v in others:
        @pl.when(there)
        def _(r=r, v=v):
            pl.semaphore_signal(barrier, inc=1, device_id=(r, v), device_id_type=MESH)
        greeted = greeted + there.astype(jnp.int32)
    pl.semaphore_wait(barrier, greeted)

    def seeds(begin):
        for dy in range(0, reach + 1):
            for mate in range(CORES):
                slot = 2 * dy + 1 - core
                target = (y + dy) * CORES + mate
                for part in range(PARTS):
                    go = jnp.logical_and(
                        slot < slots, is_carried((y + dy) % 2, mate, slot, part)
                    )
                    go = jnp.logical_and(go, y + dy < n_y)
                    go = jnp.logical_and(go, target != region)

                    @pl.when(go)
                    def _(part=part, slot=slot, target=target, dy=dy, mate=mate):
                        copy = pltpu.make_async_remote_copy(
                            src_ref=fly[part].at[0],
                            dst_ref=buf.at[slot, part, var],
                            send_sem=seed_sent.at[dy, mate, part],
                            recv_sem=recv.at[slot, part, var],
                            device_id=(target, var),
                            device_id_type=MESH,
                        )
                        if begin:
                            copy.start()
                        else:
                            copy.wait_send()

    for slot in range(slots):
        batch = 2 * y + 1 - slot
        for part in range(PARTS):
            mine = is_carried(odd, core, slot, part)

            @pl.when(jnp.logical_and(mine, batch == region))
            def _(slot=slot, part=part):
                pltpu.make_async_copy(
                    fly[part].at[0], buf.at[slot, part, var], recv.at[slot, part, var]
                ).start()

            if slot >= 2:
                @pl.when(jnp.logical_and(mine, batch < 0))
                def _(slot=slot, part=part, batch=batch):
                    pltpu.make_async_copy(
                        new[part].at[jnp.maximum(-batch - 1, 0)],
                        buf.at[slot, part, var],
                        recv.at[slot, part, var],
                    ).start()
    seeds(True)

    def wait_item(slot, part, source):
        here = buf.at[slot, part, source]
        pltpu.make_async_copy(here, here, recv.at[slot, part, source]).wait()

    def plane_unit(unit, mate):
        pairs = {key: units[min(unit, len(units) - 1)] for key, units in UNITS.items()}
        slot = choose(odd, mate, {key: pair[0] for key, pair in pairs.items()})
        part = choose(odd, mate, {key: pair[1] for key, pair in pairs.items()})
        there = choose(odd, mate, {key: unit < len(units) for key, units in UNITS.items()})
        return slot, part, there

    def shared_unit(unit, mate):
        return unit + (slots - N_SHARED) * odd, 1 - odd, mate != odd

    def keep(slot, part, source):
        if not aligned:
            return
        tick = slot - 1 + core

        @pl.when(jnp.logical_and(tick >= 0, tick < ticks))
        def _():
            high, low = split(buf[slot, part, source])
            start = pl.multiple_of(source * shard, 16)
            halves[tick, part, pl.ds(start, shard), :] = high
            halves[tick, part, pl.ds(start + obs, shard), :] = low

    def near_copy(slot, part, source, send_sem, act):
        @pl.when(jnp.where(core == 0, slot < slots - 1, slot > 0))
        def _():
            act(pltpu.make_async_remote_copy(
                src_ref=buf.at[slot, part, source],
                dst_ref=buf.at[slot, part, source],
                send_sem=send_sem,
                recv_sem=recv.at[slot, part, source],
                device_id=(region + 1 - 2 * core, var),
                device_id_type=MESH,
            ))

    def copies(unit, slot, part, z_from, x_from, act):
        source = z_from * n_x + x_from
        x_first = jnp.where(
            odd == 0,
            jnp.logical_and(slot == slots - 1, part == 1),
            jnp.logical_and(slot == 1, part == 0),
        )
        along_z = jnp.logical_or(x_first, x_from == x)
        along_x = jnp.logical_or(jnp.logical_not(x_first), z_from == z)
        up = jnp.logical_and(z_from <= z, z + 1 < n_z)
        down = jnp.logical_and(z_from >= z, z > 0)
        right = jnp.logical_and(x_from <= x, x + 1 < n_x)
        left = jnp.logical_and(x_from >= x, x > 0)
        across = is_shared(odd, slot)
        routes = [
            (jnp.logical_and(along_z, up), region, var + n_x, slot),
            (jnp.logical_and(along_z, down), region, var - n_x, slot),
            (jnp.logical_and(along_x, right), region, var + 1, slot),
            (jnp.logical_and(along_x, left), region, var - 1, slot),
            (across, region + CORES * (1 - 2 * odd), var, slot + 2 * (1 - 2 * odd)),
        ]
        for way, (go, r, v, slot_there) in enumerate(routes):
            @pl.when(go)
            def _(way=way, r=r, v=v, slot_there=slot_there):
                act(pltpu.make_async_remote_copy(
                    src_ref=buf.at[slot, part, source],
                    dst_ref=buf.at[slot_there, part, source],
                    send_sem=sent.at[unit, source, way],
                    recv_sem=recv.at[slot_there, part, source],
                    device_id=(r, v),
                    device_id_type=MESH,
                ))
        near_copy(slot, part, source, sent.at[unit, source, len(routes)], act)

    def begin(copy):
        copy.start()

    def end(copy):
        copy.wait_send()

    def ring(hop, act):
        pairs = [
            (dz, dx)
            for ax in range(min(hop, n_x - 1) + 1)
            for dz in sorted({hop - ax, ax - hop}, reverse=True)
            for dx in sorted({ax, -ax}, reverse=True)
            if hop - ax < n_z
        ]
        for dz, dx in pairs:
            z_from, x_from = z + dz, x + dx
            inside = jnp.logical_and(z_from >= 0, z_from < n_z)
            inside = jnp.logical_and(inside, jnp.logical_and(x_from >= 0, x_from < n_x))

            @pl.when(inside)
            def _(z_from=z_from, x_from=x_from):
                act(z_from, x_from)

    def gather_step(unit, hop):
        slot, part, there = plane_unit(unit, core)

        def handle(z_from, x_from):
            wait_item(slot, part, z_from * n_x + x_from)
            copies(unit, slot, part, z_from, x_from, begin)

        @pl.when(there)
        def _():
            ring(hop, handle)

    def shared_step(unit, hop):
        slot, part, there = shared_unit(unit, core)

        def handle(z_from, x_from):
            source = z_from * n_x + x_from
            wait_item(slot, part, source)
            near_copy(slot, part, source, sent.at[N_UNITS + unit, source, 0], begin)

        @pl.when(there)
        def _():
            ring(hop, handle)

    def take_step(step, mate):
        for count, lag, which in ((N_UNITS, 0, plane_unit), (N_SHARED, 1, shared_unit)):
            for unit in range(count):
                hop = step - unit - lag
                if not 0 <= hop <= far:
                    continue
                slot, part, there = which(unit, mate)
                needed = jnp.logical_and(slot - 1 + core >= 0, slot - 1 + core < ticks)

                def take(z_from, x_from, slot=slot, part=part):
                    source = z_from * n_x + x_from
                    if mate is not core:
                        wait_item(slot, part, source)
                    keep(slot, part, source)

                @pl.when(jnp.logical_and(there, needed))
                def _(hop=hop, take=take):
                    ring(hop, take)

    per_chunk = 2 if mask_ref.shape[2] % 2 == 0 else 1
    n_chunks = mask_ref.shape[2] // per_chunk
    height = per_chunk * block

    def prepare(tick, parts=range(PARTS)):
        if aligned:
            return
        slot = tick + 1 - core
        for part in parts:
            for source in range(n_var):
                stage[pl.ds(source * shard, shard), :] = buf[slot, part, source]
            high, low = split(stage[...])
            halves[tick, part, :obs, :] = high
            halves[tick, part, obs:, :] = low

    def weigh(tick, c):
        rows = pl.ds(pl.multiple_of(c * height, height), height)
        rows_in = out_ref[rows, :]
        high, low = split(rows_in)
        pair = dot(high, halves[tick, 0], NT)
        covar = pair[:, :obs] + (pair[:, obs:] + dot(low, halves[tick, 0, :obs, :], NT))
        taper_now = taper_ref[tick, rows, :].astype(jnp.float32)
        n_obs_blocks = mask_ref.shape[0]
        width = covar.shape[1] // n_obs_blocks
        strips = []
        for a in range(per_chunk):
            lines = slice(a * block, (a + 1) * block)
            pieces = []
            for b in range(n_obs_blocks):
                flag = mask_ref[b, tick, c * per_chunk + a].astype(jnp.float32)
                flag = flag * (1.0 / (members - 1))
                cols = slice(b * width, (b + 1) * width)
                pieces.append(taper_now[lines, cols] * covar[lines, cols] * flag)
            strips.append(jnp.concatenate(pieces, 1))
        weights = jnp.concatenate(strips, 0)
        return split(weights)

    def apply(tick, c, high, low):
        rows = pl.ds(pl.multiple_of(c * height, height), height)
        gain = dot(jnp.concatenate([high, high], 1), halves[tick, 1], NN)
        gain = gain + dot(low, halves[tick, 1, :obs, :], NN)
        out_ref[rows, :] = out_ref[rows, :] + gain

    def tick_now(tick):
        prepare(tick)

        def body(c, carry):
            apply(tick, c, *weigh(tick, c))
            return carry

        lax.fori_loop(0, n_chunks, body, 0)

    last_step = N_UNITS - 1 + far
    other = 1 - core
    for unit in range(AHEAD):
        gather_step(unit, 0)
    for step in range(last_step + 1):
        if step + AHEAD < N_UNITS:
            gather_step(step + AHEAD, 0)
        for unit in range(N_UNITS):
            if 1 <= step - unit <= far:
                gather_step(unit, step - unit)
        for unit in range(N_SHARED):
            if 0 <= step - unit - 1 <= far:
                shared_step(unit, step - unit - 1)
        if 0 < step < last_step:
            take_step(step - 1, core)
        if LAG <= step < last_step - 1:
            take_step(step - LAG, other)
        if step == last_step - 1:
            take_step(step, core)
            for taken in range(step - LAG, last_step):
                take_step(taken, other)
            state_load.wait()
            taper_load.wait()
            mask_load.wait()

            tick_now(0)
            prepare(1, (0,))

            def weigh_next(c, carry):
                rows = pl.ds(pl.multiple_of(c * height, height), height)
                ready[0, rows, :], ready[1, rows, :] = weigh(1, c)
                return carry

            lax.fori_loop(0, n_chunks, weigh_next, 0)
        elif step == last_step:
            take_step(step, core)
            take_step(step, other)

    def later(tick, carry):
        tick_now(tick)
        return carry

    def apply_ready(c, carry):
        rows = pl.ds(pl.multiple_of(c * height, height), height)
        apply(1, c, ready[0, rows, :], ready[1, rows, :])
        return carry

    prepare(1, (1,))
    lax.fori_loop(0, n_chunks, apply_ready, 0)
    lax.fori_loop(2, ticks, later, 0)

    seeds(False)
    for unit in range(N_UNITS):
        slot, part, there = plane_unit(unit, core)

        def left(source, carry, unit=unit, slot=slot, part=part):
            copies(unit, slot, part, source // n_x, source % n_x, end)
            return carry

        @pl.when(there)
        def _(left=left):
            lax.fori_loop(0, n_var, left, 0)
    for unit in range(N_SHARED):
        slot, part, there = shared_unit(unit, core)

        def gone(source, carry, unit=unit, slot=slot, part=part):
            near_copy(slot, part, source, sent.at[N_UNITS + unit, source, 0], end)
            return carry

        @pl.when(there)
        def _(gone=gone):
            lax.fori_loop(0, n_var, gone, 0)


def on_device(n_region, n_var, state, taper, block_mask, anom_fly, incr_fly, anom_new, incr_new):
    ticks = taper.shape[0]
    shard, members = anom_fly.shape[1:]
    obs = shard * n_var
    n_x = 2 ** (int(math.log2(n_var)) // 2)
    slots = ticks + 1
    block_mask = jnp.transpose(block_mask, (2, 0, 1))
    vmem = pl.BlockSpec(memory_space=pltpu.VMEM)
    anywhere = pl.BlockSpec(memory_space=pl.ANY)
    flops = 3 * 4 * ticks * state.shape[0] * obs * members
    return pl.pallas_call(
        functools.partial(kernel, n_region, n_var, n_x, ticks),
        out_shape=jax.ShapeDtypeStruct(state.shape, jnp.float32),
        in_specs=[anywhere] * 7,
        out_specs=vmem,
        scratch_shapes=[
            pltpu.VMEM((slots, PARTS, n_var, shard, members), jnp.float32),
            pltpu.VMEM(taper.shape, taper.dtype),
            pltpu.SMEM(block_mask.shape, block_mask.dtype),
            pltpu.VMEM((2, state.shape[0], obs), jnp.bfloat16),
            pltpu.VMEM((ticks, PARTS, 2 * obs, members), jnp.bfloat16),
            pltpu.VMEM((8, 128) if shard % 16 == 0 else (obs, members), jnp.float32),
            pltpu.SemaphoreType.DMA((slots, PARTS, n_var)),
            pltpu.SemaphoreType.DMA((N_UNITS + N_SHARED, n_var, 6)),
            pltpu.SemaphoreType.DMA((3, CORES, PARTS)),
            pltpu.SemaphoreType.DMA((3,)),
        ],
        compiler_params=pltpu.CompilerParams(
            collective_id=0, has_side_effects=True, vmem_limit_bytes=60 * 1024 * 1024
        ),
        cost_estimate=pl.CostEstimate(
            flops=flops, bytes_accessed=4 * state.size * 4, transcendentals=0
        ),
        name="gather_and_assimilate",
    )(block_mask, state, taper, anom_fly, incr_fly, anom_new, incr_new)


def solution(mesh):
    n_region, n_var = mesh.shape["region"], mesh.shape["var"]
    in_specs = (
        P(("region", "var"), None),
        P(None, ("region", "var"), None),
        P(None, ("region", "var"), None),
        P("region", "var", None),
        P("region", "var", None),
        P(None, "var", None),
        P(None, "var", None),
    )
    out_specs = P(("region", "var"), None)
    return jax.shard_map(
        functools.partial(on_device, n_region, n_var),
        mesh=mesh, in_specs=in_specs, out_specs=out_specs, check_vma=False,
    )
```
